512 devices in a mesh: blk: 16 (over y, z_hi, core), uly: 32 (over x, z_lo).
Axes of the slice: x: 4, y: 4, z: 16 (z_hi: 2, z_lo: 8; z = z_hi * 8 + z_lo), core: 2. Of those that a mesh axis runs over, the one named last changes fastest.
Arguments:
- queries: bfloat16 [4096, 1024], P(('blk', 'uly')), may hold values from -12 to 12
- keys: bfloat16 [65536, 1024], P(('blk', 'uly')), may hold values from -6 to 6
- values: bfloat16 [65536, 1024], P(('blk', 'uly')), may hold values from -6 to 6
- w_out: bfloat16 [1024, 1024], replicated, may hold values from -0.1875 to 0.1875
Outputs:
- projected: bfloat16 [4096, 1024], P(('blk', 'uly'))
The draws below stay inside these ranges and needn't reach their ends.
All inputs are finite; a program needn't handle non-finite values.
Results may differ from the reference program's by a relative error of at most 0.02.
Values may be sent and summed in bfloat16 or wider, within the bound.
No kernel may reach another device: no remote copies, remote signals or barrier semaphores. Data moves between devices by JAX's collectives and lax.ppermute only.
A program may use at most 64 MiB of HBM per device.

```python
import math
import jax
import jax.numpy as jnp
from jax import lax

D = 1024
H = 16
HD = 64
QTOK = 4096
KTOK = 65536


def draw_queries(key, part):
    key = jax.random.fold_in(key, 1)
    drawn = jnp.clip(3.0 * jax.random.normal(key, (QTOK, D), jnp.float32), -12.0, 12.0)
    return drawn.astype(jnp.bfloat16)


def draw_keys(key, part):
    key = jax.random.fold_in(key, 2)
    drawn = jnp.clip(jax.random.normal(key, (KTOK, D), jnp.float32), -6.0, 6.0)
    return drawn.astype(jnp.bfloat16)


def block_levels(rng, extent, pieces, least, largest):
    gain, own = 1.0, jax.random.fold_in(rng, 6)
    for position, parts in pieces:
        steps = jnp.exp(jax.random.uniform(jax.random.fold_in(own, position), (parts,), jnp.float32, least / len(pieces), largest / len(pieces)))
        gain = gain * jnp.repeat(steps, extent[position] // parts).reshape([-1 if axis == position else 1 for axis in range(len(extent))])
    return gain


def normal_values(key, dims, scale, bound, cuts=(), held_as=jnp.bfloat16):
    loudness = block_levels(key, dims, cuts, -0.22, 0.18) if cuts else 1.0
    entries = jax.random.normal(key, dims, jnp.float32) * scale * loudness
    return jnp.minimum(jnp.maximum(entries, -bound), bound).astype(held_as)


def setup_inputs(seed: int = 0) -> dict:
    seeds = jax.random.split(jax.random.key(seed), 5)
    queries = draw_queries(jax.random.fold_in(seeds[4], 71), 0)
    keys = draw_keys(jax.random.fold_in(seeds[4], 71), 0)
    values = normal_values(seeds[2], (KTOK, D), 1.0, 6.0, ((0, 512),))
    w_out = normal_values(seeds[3], (D, D), D ** -0.5, 0.1875)
    return {"queries": queries, "keys": keys, "values": values, "w_out": w_out}


def attend_head(q_head, k_head, v_head):
    block_rows = math.gcd(QTOK, 256)

    def one_block(q_part):
        score = jnp.dot(q_part, k_head.T, preferred_element_type=jnp.float32) * (HD ** -0.5)
        top = jnp.max(score, axis=1, keepdims=True)
        weights = jnp.exp(score - top)
        total = jnp.sum(weights, axis=1, keepdims=True)
        mixed = jnp.dot(weights.astype(jnp.bfloat16), v_head, preferred_element_type=jnp.float32)
        return (mixed / total).astype(jnp.bfloat16)

    blocks = q_head.reshape(QTOK // block_rows, block_rows, HD)
    return lax.map(one_block, blocks).reshape(QTOK, HD)


def reference(queries, keys, values, w_out):
    q_heads = queries.reshape(QTOK, H, HD).transpose(1, 0, 2)
    k_heads = keys.reshape(KTOK, H, HD).transpose(1, 0, 2)
    v_heads = values.reshape(KTOK, H, HD).transpose(1, 0, 2)
    attended = lax.map(lambda items: attend_head(items[0], items[1], items[2]), (q_heads, k_heads, v_heads))
    attended = attended.transpose(1, 0, 2).reshape(QTOK, D)
    return jnp.dot(attended, w_out, preferred_element_type=jnp.float32).astype(jnp.bfloat16)
```

```python
import functools

import jax
import jax.numpy as jnp
from jax import lax
from jax.experimental import pallas as pl
from jax.experimental.pallas import tpu as pltpu
from jax.sharding import Mesh, PartitionSpec as P

HD = 64
HEADS = 16
PLANES = 16
ALL = ("y", "zh", "core", "x", "zl")
PLANE = ("y", "x")
DEPTH = ("zh", "zl")
F32 = jnp.float32
BF16 = jnp.bfloat16
VMEM = pl.BlockSpec(memory_space=pltpu.VMEM)


def lane_of(shape):
    return lax.broadcasted_iota(jnp.int32, shape, len(shape) - 1)


def pair_kv_kernel(k_ref, v_ref, out_ref):
    low = lane_of((128, 128)) < HD
    for pair in range(HEADS // 2):
        k = k_ref[:, pair * 128 : (pair + 1) * 128]
        v = v_ref[:, pair * 128 : (pair + 1) * 128]
        k_turned = pltpu.roll(k.astype(F32), HD, 1).astype(BF16)
        v_turned = pltpu.roll(v.astype(F32), HD, 1).astype(BF16)
        out_ref[2 * pair] = jnp.where(low, k, v_turned)
        out_ref[2 * pair + 1] = jnp.where(low, k_turned, v)


def pair_kv(k, v):
    return pl.pallas_call(
        pair_kv_kernel,
        out_shape=jax.ShapeDtypeStruct((HEADS, 128, 128), BF16),
        in_specs=[VMEM, VMEM],
        out_specs=VMEM,
        name="pair_kv",
    )(k, v)


def attend_kernel(q_tile, k_tile, q_ref, ka_ref, kb_ref, out_ref, va, vb):
    low = lane_of(ka_ref.shape) < HD
    va[...] = jnp.where(low, jnp.ones((), BF16), ka_ref[...])
    vb[...] = jnp.where(low, jnp.ones((), BF16), kb_ref[...])
    rows = ka_ref.shape[0]
    blocks = q_tile // 128
    low64 = lane_of((64, 128)) < HD

    def body(step, carry):
        parts = []
        for j in range(blocks):
            pair = q_ref[step * blocks + j].astype(F32) * HD**-0.5
            parts.append(jnp.where(low64, pair, 0.0))
            parts.append(jnp.where(low64, pltpu.roll(pair, HD, 1), 0.0))
        q = jnp.concatenate(parts, 0).astype(BF16)
        top, total = None, None
        for k_ref, v_ref in ((ka_ref, va), (kb_ref, vb)):
            for c in range(rows // k_tile):
                span = slice(c * k_tile, (c + 1) * k_tile)
                score = lax.dot_general(
                    q, k_ref[span], (((1,), (1,)), ((), ())), preferred_element_type=F32
                )
                here = jnp.max(score, 1, keepdims=True)
                new = here if top is None else jnp.maximum(top, here)
                weights = jnp.exp(score - new).astype(BF16)
                part = jnp.dot(weights, v_ref[span], preferred_element_type=F32)
                total = part if top is None else total * jnp.exp(top - new) + part
                top = new
        for j in range(blocks):
            span = slice(j * 128, (j + 1) * 128)
            whole = total[span]
            mixed = whole / jnp.where(lane_of(whole.shape) < HD, 1.0, pltpu.roll(whole, HD, 1))
            packed = jnp.where(low64, pltpu.roll(mixed[:64], HD, 1), mixed[64:])
            block = step * blocks + j
            out_ref[block, 0:64, :] = packed.astype(BF16)
            level = (jnp.log(whole) + top[span]).T[0:8]
            first = level.astype(BF16).astype(F32)
            second = (level - first).astype(BF16).astype(F32)
            third = level - first - second
            row = lax.broadcasted_iota(jnp.int32, (8, 128), 0)
            terms = jnp.where(row == 0, first, jnp.where(row == 1, second, third))
            out_ref[block, 64:80, :] = jnp.concatenate([terms, terms], 0).astype(BF16)
        return carry

    lax.fori_loop(0, q_ref.shape[0] // blocks, body, 0)


def attend(q, ka, kb, q_tile=1024, k_tile=512):
    n = q.shape[0]
    rows = ka.shape[0]
    return pl.pallas_call(
        functools.partial(attend_kernel, q_tile, k_tile),
        out_shape=jax.ShapeDtypeStruct((n, 80, 128), BF16),
        in_specs=[VMEM, VMEM, VMEM],
        out_specs=VMEM,
        scratch_shapes=[pltpu.VMEM(ka.shape, BF16), pltpu.VMEM(kb.shape, BF16)],
        compiler_params=pltpu.CompilerParams(vmem_limit_bytes=48 * 2**20),
        cost_estimate=pl.CostEstimate(
            flops=8 * n * 128 * rows * 128,
            bytes_accessed=2**21,
            transcendentals=2 * n * 128 * rows,
        ),
        name="attend",
    )(q, ka, kb)


def combine_kernel(part_ref, out_ref):
    n = part_ref.shape[0]
    levels = []
    for z in range(n):
        terms = part_ref[z, 64:80, :].astype(F32)
        levels.append(terms[0:1] + terms[1:2] + terms[2:3])
    level = jnp.concatenate(levels, 0)
    weight = jnp.exp(level - jnp.max(level, 0, keepdims=True))
    weight = weight / jnp.sum(weight, 0, keepdims=True)
    weight = jnp.concatenate([weight, jnp.zeros((128 - n, 128), F32)], 0).T
    low64 = lane_of((64, 128)) < HD
    total = jnp.zeros((64, 128), F32)
    for z in range(n):
        column = weight[:, z : z + 1]
        total += jnp.where(low64, column[:64], column[64:]) * part_ref[z, 0:64, :].astype(F32)
    out_ref[...] = total.astype(BF16)


def combine(parts):
    return pl.pallas_call(
        combine_kernel,
        out_shape=jax.ShapeDtypeStruct((64, 128), BF16),
        in_specs=[VMEM],
        out_specs=VMEM,
        name="combine",
    )(parts)


def exchange(blocks, axes):
    return lax.all_to_all(blocks, axes, split_axis=0, concat_axis=0, tiled=True)


def local(queries, keys, values, w_out):
    q_send = queries.reshape(2, 4, HEADS, HD).transpose(2, 1, 0, 3).reshape(HEADS, 4, 128)
    q_plane = exchange(q_send, PLANE).reshape(64, 128)
    q_all = exchange(jnp.broadcast_to(q_plane, (PLANES, 64, 128)), DEPTH)
    kv = exchange(pair_kv(keys, values), PLANE).reshape(HEADS * 128, 128)
    kv_other = lax.ppermute(kv, "core", [(0, 1), (1, 0)])
    parts = exchange(attend(q_all, kv, kv_other), DEPTH)
    attended = combine(parts).reshape(HEADS, 4, 128)
    rows = exchange(attended, PLANE).reshape(HEADS, 4, 2, HD)
    rows = rows.transpose(2, 1, 0, 3).reshape(8, HEADS * HD)
    return jnp.dot(rows, w_out, preferred_element_type=F32).astype(BF16)


def solution(mesh):
    split = Mesh(mesh.devices.reshape(4, 2, 2, 4, 8), ALL)
    return jax.shard_map(
        local,
        mesh=split,
        in_specs=(P(ALL, None), P(ALL, None), P(ALL, None), P()),
        out_specs=P(ALL, None),
        check_vma=False,
    )
```

```python
import functools

import jax
import jax.numpy as jnp
from jax import lax
from jax.experimental import pallas as pl
from jax.experimental.pallas import tpu as pltpu
from jax.sharding import Mesh, PartitionSpec as P

HD = 64
HEADS = 16
PLANES = 16
ALL = ("y", "zh", "core", "x", "zl")
PLANE = ("y", "x")
DEPTH = ("zh", "zl")
F32 = jnp.float32
BF16 = jnp.bfloat16
VMEM = pl.BlockSpec(memory_space=pltpu.VMEM)


def lane_of(shape):
    return lax.broadcasted_iota(jnp.int32, shape, len(shape) - 1)


def pack_kernel(q_ref, k_ref, v_ref, out_ref):
    low = lane_of((128, 128)) < HD
    low4 = lane_of((4, 128)) < HD
    rest = jnp.zeros((12, 128), F32)
    for pair in range(HEADS // 2):
        span = slice(pair * 128, (pair + 1) * 128)
        k = k_ref[:, span]
        v = v_ref[:, span]
        k_turned = pltpu.roll(k.astype(F32), HD, 1).astype(BF16)
        v_turned = pltpu.roll(v.astype(F32), HD, 1).astype(BF16)
        out_ref[2 * pair, 0:128, :] = jnp.where(low, k, v_turned)
        out_ref[2 * pair + 1, 0:128, :] = jnp.where(low, k_turned, v)
        q = q_ref[:, span].astype(F32)
        q_turned = pltpu.roll(q, HD, 1)
        even = jnp.where(low4, q[0:4], q_turned[4:8])
        odd = jnp.where(low4, q_turned[0:4], q[4:8])
        out_ref[2 * pair, 128:144, :] = jnp.concatenate([even, rest], 0).astype(BF16)
        out_ref[2 * pair + 1, 128:144, :] = jnp.concatenate([odd, rest], 0).astype(BF16)


def pack(q, k, v):
    return pl.pallas_call(
        pack_kernel,
        out_shape=jax.ShapeDtypeStruct((HEADS, 144, 128), BF16),
        in_specs=[VMEM, VMEM, VMEM],
        out_specs=VMEM,
        name="pack",
    )(q, k, v)


def attend_kernel(q_tile, k_tile, q_ref, kva_ref, kvb_ref, out_ref, ka_ref, va, kb_ref, vb):
    low = lane_of((128, 128)) < HD
    for source in range(HEADS):
        span = slice(source * 128, (source + 1) * 128)
        for kv_ref, k_ref, v_ref in ((kva_ref, ka_ref, va), (kvb_ref, kb_ref, vb)):
            block = kv_ref[source, 0:128, :]
            k_ref[span] = block
            v_ref[span] = jnp.where(low, jnp.ones((), BF16), block)
    rows = ka_ref.shape[0]
    blocks = q_tile // 128
    low64 = lane_of((64, 128)) < HD

    def body(step, carry):
        parts = []
        for j in range(blocks):
            pair = q_ref[step * blocks + j].astype(F32) * HD**-0.5
            parts.append(jnp.where(low64, pair, 0.0))
            parts.append(jnp.where(low64, pltpu.roll(pair, HD, 1), 0.0))
        q = jnp.concatenate(parts, 0).astype(BF16)
        top, total = None, None
        for k_ref, v_ref in ((ka_ref, va), (kb_ref, vb)):
            for c in range(rows // k_tile):
                span = slice(c * k_tile, (c + 1) * k_tile)
                score = lax.dot_general(
                    q, k_ref[span], (((1,), (1,)), ((), ())), preferred_element_type=F32
                )
                here = jnp.max(score, 1, keepdims=True)
                new = here if top is None else jnp.maximum(top, here)
                weights = jnp.exp(score - new).astype(BF16)
                part = jnp.dot(weights, v_ref[span], preferred_element_type=F32)
                total = part if top is None else total * jnp.exp(top - new) + part
                top = new
        for j in range(blocks):
            span = slice(j * 128, (j + 1) * 128)
            whole = total[span]
            mixed = whole / jnp.where(lane_of(whole.shape) < HD, 1.0, pltpu.roll(whole, HD, 1))
            packed = jnp.where(low64, pltpu.roll(mixed[:64], HD, 1), mixed[64:])
            block = step * blocks + j
            out_ref[block, 0:64, :] = packed.astype(BF16)
            level = (jnp.log(whole) + top[span]).T[0:8]
            first = level.astype(BF16).astype(F32)
            second = (level - first).astype(BF16).astype(F32)
            third = level - first - second
            row = lax.broadcasted_iota(jnp.int32, (8, 128), 0)
            terms = jnp.where(row == 0, first, jnp.where(row == 1, second, third))
            out_ref[block, 64:80, :] = jnp.concatenate([terms, terms], 0).astype(BF16)
        return carry

    lax.fori_loop(0, q_ref.shape[0] // blocks, body, 0)


def attend(q, kva, kvb, q_tile=1024, k_tile=512):
    n = q.shape[0]
    rows = HEADS * 128
    return pl.pallas_call(
        functools.partial(attend_kernel, q_tile, k_tile),
        out_shape=jax.ShapeDtypeStruct((n, 80, 128), BF16),
        in_specs=[VMEM, VMEM, VMEM],
        out_specs=VMEM,
        scratch_shapes=[pltpu.VMEM((rows, 128), BF16)] * 4,
        compiler_params=pltpu.CompilerParams(vmem_limit_bytes=48 * 2**20),
        cost_estimate=pl.CostEstimate(
            flops=8 * n * 128 * rows * 128,
            bytes_accessed=2**21,
            transcendentals=2 * n * 128 * rows,
        ),
        name="attend",
    )(q, kva, kvb)


def combine_kernel(part_ref, out_ref):
    n = part_ref.shape[0]
    levels = []
    for z in range(n):
        terms = part_ref[z, 64:80, :].astype(F32)
        levels.append(terms[0:1] + terms[1:2] + terms[2:3])
    level = jnp.concatenate(levels, 0)
    weight = jnp.exp(level - jnp.max(level, 0, keepdims=True))
    weight = weight / jnp.sum(weight, 0, keepdims=True)
    weight = jnp.concatenate([weight, jnp.zeros((128 - n, 128), F32)], 0).T
    low64 = lane_of((64, 128)) < HD
    total = jnp.zeros((64, 128), F32)
    for z in range(n):
        column = weight[:, z : z + 1]
        total += jnp.where(low64, column[:64], column[64:]) * part_ref[z, 0:64, :].astype(F32)
    out_ref[...] = total.astype(BF16)


def combine(parts):
    return pl.pallas_call(
        combine_kernel,
        out_shape=jax.ShapeDtypeStruct((64, 128), BF16),
        in_specs=[VMEM],
        out_specs=VMEM,
        name="combine",
    )(parts)


def exchange(blocks, axes):
    return lax.all_to_all(blocks, axes, split_axis=0, concat_axis=0, tiled=True)


def local(queries, keys, values, w_out):
    held = exchange(pack(queries, keys, values), PLANE)
    held_other = lax.ppermute(held, "core", [(0, 1), (1, 0)])
    q_plane = held[:, 128:132, :].reshape(1, 64, 128)
    q_all = exchange(jnp.broadcast_to(q_plane, (PLANES, 64, 128)), DEPTH)
    parts = exchange(attend(q_all, held, held_other), DEPTH)
    attended = combine(parts).reshape(HEADS, 4, 128)
    rows = exchange(attended, PLANE).reshape(HEADS, 4, 2, HD)
    rows = rows.transpose(2, 1, 0, 3).reshape(8, HEADS * HD)
    return jnp.dot(rows, w_out, preferred_element_type=F32).astype(BF16)


def solution(mesh):
    split = Mesh(mesh.devices.reshape(4, 2, 2, 4, 8), ALL)
    return jax.shard_map(
        local,
        mesh=split,
        in_specs=(P(ALL, None), P(ALL, None), P(ALL, None), P()),
        out_specs=P(ALL, None),
        check_vma=False,
    )
```

```python
import functools

import jax
import jax.numpy as jnp
from jax import lax
from jax.experimental import pallas as pl
from jax.experimental.pallas import tpu as pltpu
from jax.sharding import Mesh, PartitionSpec as P

HD = 64
HEADS = 16
STEPS = 8
ALL = ("y", "zh", "core", "xa", "xb", "zq", "zo")
PLACE = ("y", "xa", "zo")
DEPTH = ("zh", "zq")
F32 = jnp.float32
BF16 = jnp.bfloat16
VMEM = pl.BlockSpec(memory_space=pltpu.VMEM)


def iota(shape, dim):
    return lax.broadcasted_iota(jnp.int32, shape, dim)


def pack_kernel(q_ref, k_ref, v_ref, out_ref):
    low = iota((128, 128), 1) < HD
    low4 = iota((4, 128), 1) < HD
    rest = jnp.zeros((12, 128), F32)
    for pair in range(HEADS // 2):
        span = slice(pair * 128, (pair + 1) * 128)
        k = k_ref[:, span]
        v = v_ref[:, span]
        k_turned = pltpu.roll(k.astype(F32), HD, 1).astype(BF16)
        v_turned = pltpu.roll(v.astype(F32), HD, 1).astype(BF16)
        out_ref[2 * pair, 0:128, :] = jnp.where(low, k, v_turned)
        out_ref[2 * pair + 1, 0:128, :] = jnp.where(low, k_turned, v)
        q = q_ref[:, span].astype(F32)
        q_turned = pltpu.roll(q, HD, 1)
        even = jnp.where(low4, q[0:4], q_turned[4:8])
        odd = jnp.where(low4, q_turned[0:4], q[4:8])
        out_ref[2 * pair, 128:144, :] = jnp.concatenate([even, rest], 0).astype(BF16)
        out_ref[2 * pair + 1, 128:144, :] = jnp.concatenate([odd, rest], 0).astype(BF16)


def pack(q, k, v):
    return pl.pallas_call(
        pack_kernel,
        out_shape=jax.ShapeDtypeStruct((HEADS, 144, 128), BF16),
        in_specs=[VMEM, VMEM, VMEM],
        out_specs=VMEM,
        name="pack",
    )(q, k, v)


def attend_kernel(group, q_ref, *refs):
    kv_refs, out_ref = refs[:4], refs[4]
    low64 = iota((64, 128), 1) < HD
    rows = group * 128
    low = iota((rows, 128), 1) < HD
    parts = []
    for step in range(STEPS):
        pair = q_ref[step].astype(F32) * HD**-0.5
        parts.append(jnp.where(low64, pair, 0.0))
        parts.append(jnp.where(low64, pltpu.roll(pair, HD, 1), 0.0))
    q = jnp.concatenate(parts, 0).astype(BF16)
    top, total = None, None
    for kv_ref in kv_refs:
        for c in range(HEADS // group):
            kv = kv_ref[c * group : (c + 1) * group, 0:128, :].reshape(rows, 128)
            score = lax.dot_general(
                q, kv, (((1,), (1,)), ((), ())), preferred_element_type=F32
            )
            here = jnp.max(score, 1, keepdims=True)
            new = here if top is None else jnp.maximum(top, here)
            weights = jnp.exp(score - new).astype(BF16)
            marked = jnp.where(low, jnp.ones((), BF16), kv)
            part = jnp.dot(weights, marked, preferred_element_type=F32)
            total = part if top is None else total * jnp.exp(top - new) + part
            top = new
    sub = iota((64, 128), 0) % 8 < 4
    first_half = iota((64, 128), 1) % HD < HD // 2
    for step in range(STEPS):
        a = total[step * 128 : step * 128 + 64]
        b = total[step * 128 + 64 : step * 128 + 128]
        weight = jnp.where(low64, a, pltpu.roll(b, HD, 1))
        mixed = jnp.where(low64, pltpu.roll(a, HD, 1), b) / weight
        highest = jnp.where(
            low64, top[step * 128 : step * 128 + 64], top[step * 128 + 64 : step * 128 + 128]
        )
        level = jnp.log(weight) + highest
        first = level.astype(BF16).astype(F32)
        level = jnp.where(first_half, first, level - first)
        mixed_turned = pltpu.roll(mixed.reshape(8, 8, 128), 4, 1).reshape(64, 128)
        level_turned = pltpu.roll(level.reshape(8, 8, 128), 4, 1).reshape(64, 128)
        even = jnp.where(sub, mixed, level_turned).reshape(8, 8, 128)
        odd = jnp.where(sub, mixed_turned, level).reshape(8, 8, 128)
        both = jnp.stack([even, odd], 1).reshape(128, 128)
        out_ref[step * 128 : (step + 1) * 128, :] = both.astype(BF16)


def attend(q, kvs, group=2):
    rows = len(kvs) * HEADS * 128
    return pl.pallas_call(
        functools.partial(attend_kernel, group),
        out_shape=jax.ShapeDtypeStruct((STEPS * 128, 128), BF16),
        in_specs=[VMEM] * (1 + len(kvs)),
        out_specs=VMEM,
        compiler_params=pltpu.CompilerParams(vmem_limit_bytes=48 * 2**20),
        cost_estimate=pl.CostEstimate(
            flops=4 * STEPS * 128 * rows * 128,
            bytes_accessed=2**22,
            transcendentals=STEPS * 128 * rows,
        ),
        name="attend",
    )(q, *kvs)


def finish_kernel(part_ref, w_ref, out_ref):
    near = iota((HEADS * 8, 128), 1) % HD < HD // 2
    blocks, levels = [], []
    for step in range(STEPS):
        block = part_ref[step * HEADS * 8 : (step + 1) * HEADS * 8, :].astype(F32)
        other = jnp.where(near, pltpu.roll(block, 96, 1), pltpu.roll(block, 32, 1))
        level = (block + other).reshape(HEADS, 8, 128)
        blocks.append(block.reshape(HEADS, 8, 128))
        levels.append(pltpu.roll(level, 4, 1))
    top = functools.reduce(jnp.maximum, levels)
    weights = [jnp.exp(level - top) for level in levels]
    mixed = sum(w * b for w, b in zip(weights, blocks)) / sum(weights)
    turned = pltpu.roll(mixed, HD, 2)
    low = iota((8, 128), 1) < HD
    upper = iota((8, 128), 0) < 4
    tiles = []
    for pair in range(HEADS // 2):
        head = jnp.where(low, mixed[2 * pair], turned[2 * pair + 1])
        tail = jnp.where(low, turned[2 * pair], mixed[2 * pair + 1])
        tiles.append(jnp.where(upper, head, pltpu.roll(tail, 4, 0)))
    rows = jnp.concatenate(tiles, 1).astype(BF16)
    out_ref[...] = jnp.dot(rows, w_ref[...], preferred_element_type=F32).astype(BF16)


def finish(parts, w_out):
    return pl.pallas_call(
        finish_kernel,
        out_shape=jax.ShapeDtypeStruct((8, HEADS * HD), BF16),
        in_specs=[VMEM, VMEM],
        out_specs=VMEM,
        name="finish",
    )(parts, w_out)


def exchange(blocks, axes):
    return lax.all_to_all(blocks, axes, split_axis=0, concat_axis=0, tiled=True)


def swap(block, axis):
    return lax.ppermute(block, axis, [(0, 1), (1, 0)])


def local(queries, keys, values, w_out):
    held = exchange(pack(queries, keys, values), PLACE)
    held_x = swap(held, "xb")
    held_core = swap(held, "core")
    q_place = held[:, 128:132, :].reshape(1, 64, 128)
    q_all = exchange(jnp.broadcast_to(q_place, (STEPS, 64, 128)), DEPTH)
    held_x, q_all = lax.optimization_barrier((held_x, q_all))
    held_both = swap(held_x, "core")
    parts = attend(q_all, (held, held_core, held_x, held_both))
    parts = exchange(parts.reshape(STEPS * HEADS, 8, 128), DEPTH + PLACE)
    return finish(parts.reshape(STEPS * HEADS * 8, 128), w_out)


def solution(mesh):
    split = Mesh(mesh.devices.reshape(4, 2, 2, 2, 2, 4, 2), ALL)
    return jax.shard_map(
        local,
        mesh=split,
        in_specs=(P(ALL, None), P(ALL, None), P(ALL, None), P()),
        out_specs=P(ALL, None),
        check_vma=False,
    )
```

```python
import functools

import jax
import jax.numpy as jnp
from jax import lax
from jax.experimental import pallas as pl
from jax.experimental.pallas import tpu as pltpu
from jax.sharding import Mesh, PartitionSpec as P

HD = 64
HEADS = 16
NEAR = 4
FAR = 4
ALL = ("y", "far_a", "core", "x", "far_b", "near")
PLACE = ("x", "y")
DEPTH = ("near", "far_a", "far_b")
F32 = jnp.float32
BF16 = jnp.bfloat16
VMEM = pl.BlockSpec(memory_space=pltpu.VMEM)


def iota(shape, dim):
    return lax.broadcasted_iota(jnp.int32, shape, dim)


def pack_kernel(q_ref, k_ref, v_ref, out_ref):
    low = iota((128, 128), 1) < HD
    low4 = iota((4, 128), 1) < HD
    rest = jnp.zeros((12, 128), F32)
    for pair in range(HEADS // 2):
        span = slice(pair * 128, (pair + 1) * 128)
        k = k_ref[:, span]
        v = v_ref[:, span]
        k_turned = pltpu.roll(k.astype(F32), HD, 1).astype(BF16)
        v_turned = pltpu.roll(v.astype(F32), HD, 1).astype(BF16)
        out_ref[2 * pair, 0:128, :] = jnp.where(low, k, v_turned)
        out_ref[2 * pair + 1, 0:128, :] = jnp.where(low, k_turned, v)
        q = q_ref[:, span].astype(F32)
        q_turned = pltpu.roll(q, HD, 1)
        even = jnp.where(low4, q[0:4], q_turned[4:8])
        odd = jnp.where(low4, q_turned[0:4], q[4:8])
        out_ref[2 * pair, 128:144, :] = jnp.concatenate([even, rest], 0).astype(BF16)
        out_ref[2 * pair + 1, 128:144, :] = jnp.concatenate([odd, rest], 0).astype(BF16)


def pack(q, k, v):
    return pl.pallas_call(
        pack_kernel,
        out_shape=jax.ShapeDtypeStruct((HEADS, 144, 128), BF16),
        in_specs=[VMEM, VMEM, VMEM],
        out_specs=VMEM,
        name="pack",
    )(q, k, v)


def packed_stats(level):
    level = level.T[0:8]
    first = level.astype(BF16).astype(F32)
    second = (level - first).astype(BF16).astype(F32)
    third = level - first - second
    row = iota((8, 128), 0)
    terms = jnp.where(row == 0, first, jnp.where(row == 1, second, third))
    return jnp.concatenate([terms, terms], 0).astype(BF16)


def attend_kernel(blocks, group, q_ref, kva_ref, kvb_ref, out_ref):
    low16 = iota((16, 128), 1) < HD
    low64 = iota((64, 128), 1) < HD
    rows = group * 128
    low = iota((rows, 128), 1) < HD

    def body(step, carry):
        parts = []
        for j in range(blocks):
            x = step * (blocks // NEAR) + j // NEAR
            near = j % NEAR
            first, second = [], []
            for far in range(FAR):
                span = pl.ds(pl.multiple_of(x * 16, 16), 16)
                pair = q_ref[near * FAR + far, span, :].astype(F32) * HD**-0.5
                first.append(jnp.where(low16, pair, 0.0))
                second.append(jnp.where(low16, pltpu.roll(pair, HD, 1), 0.0))
            parts += first + second
        q = jnp.concatenate(parts, 0).astype(BF16)
        top, total = None, None
        for kv_ref in (kva_ref, kvb_ref):
            for c in range(HEADS // group):
                kv = kv_ref[c * group : (c + 1) * group, 0:128, :].reshape(rows, 128)
                score = lax.dot_general(
                    q, kv, (((1,), (1,)), ((), ())), preferred_element_type=F32
                )
                here = jnp.max(score, 1, keepdims=True)
                new = here if top is None else jnp.maximum(top, here)
                weights = jnp.exp(score - new).astype(BF16)
                marked = jnp.where(low, jnp.ones((), BF16), kv)
                part = jnp.dot(weights, marked, preferred_element_type=F32)
                total = part if top is None else total * jnp.exp(top - new) + part
                top = new
        for j in range(blocks):
            span = slice(j * 128, (j + 1) * 128)
            whole = total[span]
            mixed = whole / jnp.where(iota((128, 128), 1) < HD, 1.0, pltpu.roll(whole, HD, 1))
            packed = jnp.where(low64, pltpu.roll(mixed[:64], HD, 1), mixed[64:])
            block = step * blocks + j
            out_ref[block, 0:64, :] = packed.astype(BF16)
            out_ref[block, 64:80, :] = packed_stats(jnp.log(whole) + top[span])
        return carry

    lax.fori_loop(0, 16 // blocks, body, 0)


def attend(q, kva, kvb, blocks=8, group=2):
    rows = 2 * HEADS * 128
    return pl.pallas_call(
        functools.partial(attend_kernel, blocks, group),
        out_shape=jax.ShapeDtypeStruct((16, 80, 128), BF16),
        in_specs=[VMEM] * 3,
        out_specs=VMEM,
        compiler_params=pltpu.CompilerParams(vmem_limit_bytes=48 * 2**20),
        cost_estimate=pl.CostEstimate(
            flops=4 * 2048 * rows * 128, bytes_accessed=2**21, transcendentals=2048 * rows
        ),
        name="attend",
    )(q, kva, kvb)


def gather_near_kernel(part_ref, out_ref):
    rows, sums = [], []
    for x in range(4):
        levels = []
        for near in range(NEAR):
            terms = part_ref[x * NEAR + near, 64:80, :].astype(F32)
            levels.append(terms[0:1] + terms[1:2] + terms[2:3])
        top = functools.reduce(jnp.maximum, levels)
        weights = [jnp.exp(level - top) for level in levels]
        whole = sum(weights)
        rows += [weight / whole for weight in weights]
        sums.append(top + jnp.log(whole))
    table = jnp.concatenate(rows + sums + [jnp.zeros((108, 128), F32)], 0).T
    low64 = iota((64, 128), 1) < HD
    sub = iota((64, 128), 0) % 8 < 4
    first_half = iota((64, 128), 1) % HD < HD // 2

    def column(n):
        c = table[:, n : n + 1]
        return jnp.where(low64, c[:64], c[64:])

    heads = []
    for x in range(4):
        mixed = sum(
            column(x * NEAR + near) * part_ref[x * NEAR + near, 0:64, :].astype(F32)
            for near in range(NEAR)
        )
        level = column(16 + x)
        first = level.astype(BF16).astype(F32)
        level = jnp.where(first_half, first, level - first)
        mixed_turned = pltpu.roll(mixed.reshape(8, 8, 128), 4, 1).reshape(64, 128)
        level_turned = pltpu.roll(level.reshape(8, 8, 128), 4, 1).reshape(64, 128)
        even = jnp.where(sub, mixed, level_turned)
        odd = jnp.where(sub, mixed_turned, level)
        heads.append((even, odd))
    for owner in range(16):
        span = slice(owner // 2 * 8, owner // 2 * 8 + 8)
        tiles = [heads[x][owner % 2][span] for x in range(4)]
        out_ref[owner] = jnp.concatenate(tiles, 0).astype(BF16)


def gather_near(parts):
    return pl.pallas_call(
        gather_near_kernel,
        out_shape=jax.ShapeDtypeStruct((16, 32, 128), BF16),
        in_specs=[VMEM],
        out_specs=VMEM,
        name="gather_near",
    )(parts)


def finish_kernel(part_ref, w_hbm, out_ref, w_ref, sem):
    copy = pltpu.make_async_copy(w_hbm, w_ref, sem)
    copy.start()
    near = iota((HEADS * 8, 128), 1) % HD < HD // 2
    blocks, levels = [], []
    for far in range(FAR):
        block = part_ref[far * 4 : (far + 1) * 4].reshape(HEADS * 8, 128).astype(F32)
        other = jnp.where(near, pltpu.roll(block, 96, 1), pltpu.roll(block, 32, 1))
        level = (block + other).reshape(HEADS, 8, 128)
        blocks.append(block.reshape(HEADS, 8, 128))
        levels.append(pltpu.roll(level, 4, 1))
    top = functools.reduce(jnp.maximum, levels)
    weights = [jnp.exp(level - top) for level in levels]
    mixed = sum(w * b for w, b in zip(weights, blocks)) / sum(weights)
    turned = pltpu.roll(mixed, HD, 2)
    low = iota((8, 128), 1) < HD
    upper = iota((8, 128), 0) < 4
    tiles = []
    for pair in range(HEADS // 2):
        a, b = (h % 4 * 4 + h // 4 for h in (2 * pair, 2 * pair + 1))
        head = jnp.where(low, mixed[a], turned[b])
        tail = jnp.where(low, turned[a], mixed[b])
        tiles.append(jnp.where(upper, head, pltpu.roll(tail, 4, 0)))
    rows = jnp.concatenate(tiles, 1).astype(BF16)
    copy.wait()
    out_ref[...] = jnp.dot(rows, w_ref[...], preferred_element_type=F32).astype(BF16)


def finish(parts, w_out):
    return pl.pallas_call(
        finish_kernel,
        out_shape=jax.ShapeDtypeStruct((8, HEADS * HD), BF16),
        in_specs=[VMEM, pl.BlockSpec(memory_space=pl.ANY)],
        out_specs=VMEM,
        scratch_shapes=[pltpu.VMEM(w_out.shape, BF16), pltpu.SemaphoreType.DMA],
        name="finish",
    )(parts, w_out)


def exchange(blocks, axes):
    return lax.all_to_all(blocks, axes, split_axis=0, concat_axis=0, tiled=True)


def local(queries, keys, values, w_out):
    held = exchange(pack(queries, keys, values), PLACE)
    held_core = lax.ppermute(held, "core", [(0, 1), (1, 0)])
    q_place = held[:, 128:132, :].reshape(1, 64, 128)
    q_all = exchange(jnp.broadcast_to(q_place, (16, 64, 128)), DEPTH)
    parts = exchange(attend(q_all, held, held_core), ("x", "near"))
    parts = exchange(gather_near(parts), ("far_a", "far_b", "y"))
    return finish(parts, w_out)


def solution(mesh):
    split = Mesh(mesh.devices.reshape(4, 2, 2, 4, 2, 4), ALL)
    return jax.shard_map(
        local,
        mesh=split,
        in_specs=(P(ALL, None), P(ALL, None), P(ALL, None), P()),
        out_specs=P(ALL, None),
        check_vma=False,
    )
```

```python
import functools

import jax
import jax.numpy as jnp
from jax import lax
from jax.experimental import pallas as pl
from jax.experimental.pallas import tpu as pltpu
from jax.sharding import Mesh, PartitionSpec as P

HD = 64
HEADS = 16
STEPS = 8
ALL = ("y", "zh", "core", "xa", "xb", "zq", "zo")
SPREAD = ("y", "xa", "zo", "xb")
PLACE = ("y", "xa", "zo")
DEPTH = ("zh", "zq")
F32 = jnp.float32
BF16 = jnp.bfloat16
VMEM = pl.BlockSpec(memory_space=pltpu.VMEM)


def iota(shape, dim):
    return lax.broadcasted_iota(jnp.int32, shape, dim)


def pack_kernel(q_ref, k_ref, v_ref, out_ref):
    low = iota((128, 128), 1) < HD
    low4 = iota((4, 128), 1) < HD
    rest = jnp.zeros((12, 128), F32)
    for pair in range(HEADS // 2):
        span = slice(pair * 128, (pair + 1) * 128)
        k = k_ref[:, span]
        v = v_ref[:, span]
        k_turned = pltpu.roll(k.astype(F32), HD, 1).astype(BF16)
        v_turned = pltpu.roll(v.astype(F32), HD, 1).astype(BF16)
        even_kv = jnp.where(low, k, v_turned)
        odd_kv = jnp.where(low, k_turned, v)
        q = q_ref[:, span].astype(F32)
        q_turned = pltpu.roll(q, HD, 1)
        even = jnp.where(low4, q[0:4], q_turned[4:8])
        odd = jnp.where(low4, q_turned[0:4], q[4:8])
        even = jnp.concatenate([even, rest], 0).astype(BF16)
        odd = jnp.concatenate([odd, rest], 0).astype(BF16)
        for half in range(2):
            out_ref[4 * pair + half, 0:128, :] = even_kv
            out_ref[4 * pair + half, 128:144, :] = even
            out_ref[4 * pair + 2 + half, 0:128, :] = odd_kv
            out_ref[4 * pair + 2 + half, 128:144, :] = odd


def pack(q, k, v):
    return pl.pallas_call(
        pack_kernel,
        out_shape=jax.ShapeDtypeStruct((2 * HEADS, 144, 128), BF16),
        in_specs=[VMEM, VMEM, VMEM],
        out_specs=VMEM,
        name="pack",
    )(q, k, v)


def attend_kernel(group, q_ref, *refs):
    kv_refs, out_ref = refs[:-1], refs[-1]
    low64 = iota((64, 128), 1) < HD
    rows = group * 128
    low = iota((rows, 128), 1) < HD
    parts = []
    for step in range(STEPS):
        pair = q_ref[step].astype(F32) * HD**-0.5
        parts.append(jnp.where(low64, pair, 0.0))
        parts.append(jnp.where(low64, pltpu.roll(pair, HD, 1), 0.0))
    q = jnp.concatenate(parts, 0).astype(BF16)
    top, total = None, None
    for kv_ref in kv_refs:
        for c in range(kv_ref.shape[0] // group):
            kv = kv_ref[c * group : (c + 1) * group, 0:128, :].reshape(rows, 128)
            score = lax.dot_general(
                q, kv, (((1,), (1,)), ((), ())), preferred_element_type=F32
            )
            here = jnp.max(score, 1, keepdims=True)
            new = here if top is None else jnp.maximum(top, here)
            weights = jnp.exp(score - new).astype(BF16)
            marked = jnp.where(low, jnp.ones((), BF16), kv)
            part = jnp.dot(weights, marked, preferred_element_type=F32)
            total = part if top is None else total * jnp.exp(top - new) + part
            top = new
    sub = iota((64, 128), 0) % 8 < 4
    first_half = iota((64, 128), 1) % HD < HD // 2
    for step in range(STEPS):
        a = total[step * 128 : step * 128 + 64]
        b = total[step * 128 + 64 : step * 128 + 128]
        weight = jnp.where(low64, a, pltpu.roll(b, HD, 1))
        mixed = jnp.where(low64, pltpu.roll(a, HD, 1), b) / weight
        highest = jnp.where(
            low64, top[step * 128 : step * 128 + 64], top[step * 128 + 64 : step * 128 + 128]
        )
        level = jnp.log(weight) + highest
        first = level.astype(BF16).astype(F32)
        level = jnp.where(first_half, first, level - first)
        mixed_turned = pltpu.roll(mixed.reshape(8, 8, 128), 4, 1).reshape(64, 128)
        level_turned = pltpu.roll(level.reshape(8, 8, 128), 4, 1).reshape(64, 128)
        even = jnp.where(sub, mixed, level_turned).reshape(8, 8, 128)
        odd = jnp.where(sub, mixed_turned, level).reshape(8, 8, 128)
        both = jnp.stack([even, odd], 1).reshape(128, 128)
        out_ref[step * 128 : (step + 1) * 128, :] = both.astype(BF16)


def attend(q, kvs, group=2):
    rows = 128 * sum(kv.shape[0] for kv in kvs)
    return pl.pallas_call(
        functools.partial(attend_kernel, group),
        out_shape=jax.ShapeDtypeStruct((STEPS * 128, 128), BF16),
        in_specs=[VMEM] * (1 + len(kvs)),
        out_specs=VMEM,
        compiler_params=pltpu.CompilerParams(vmem_limit_bytes=32 * 2**20),
        cost_estimate=pl.CostEstimate(
            flops=4 * STEPS * 128 * rows * 128,
            bytes_accessed=2**22,
            transcendentals=STEPS * 128 * rows,
        ),
        name="attend",
    )(q, *kvs)


def finish_kernel(part_ref, out_ref):
    near = iota((HEADS * 8, 128), 1) % HD < HD // 2
    blocks, levels = [], []
    for step in range(STEPS):
        block = part_ref[step * HEADS * 8 : (step + 1) * HEADS * 8, :].astype(F32)
        other = jnp.where(near, pltpu.roll(block, 96, 1), pltpu.roll(block, 32, 1))
        level = (block + other).reshape(HEADS, 8, 128)
        blocks.append(block.reshape(HEADS, 8, 128))
        levels.append(pltpu.roll(level, 4, 1))
    top = functools.reduce(jnp.maximum, levels)
    weights = [jnp.exp(level - top) for level in levels]
    mixed = sum(w * b for w, b in zip(weights, blocks)) / sum(weights)
    turned = pltpu.roll(mixed, HD, 2)
    low = iota((8, 128), 1) < HD
    upper = iota((8, 128), 0) < 4
    tiles = []
    for pair in range(HEADS // 2):
        head = jnp.where(low, mixed[2 * pair], turned[2 * pair + 1])
        tail = jnp.where(low, turned[2 * pair], mixed[2 * pair + 1])
        tiles.append(jnp.where(upper, head, pltpu.roll(tail, 4, 0)))
    out_ref[...] = jnp.concatenate(tiles, 1).astype(BF16)


def finish(parts):
    return pl.pallas_call(
        finish_kernel,
        out_shape=jax.ShapeDtypeStruct((8, HEADS * HD), BF16),
        in_specs=[VMEM],
        out_specs=VMEM,
        name="finish",
    )(parts)


def exchange(blocks, axes):
    return lax.all_to_all(blocks, axes, split_axis=0, concat_axis=0, tiled=True)


def local(queries, keys, values, w_out):
    held = exchange(pack(queries, keys, values), SPREAD)
    held_core = lax.ppermute(held, "core", [(0, 1), (1, 0)])
    own = lax.dynamic_slice(
        held.reshape(HEADS, 2, 144, 128), (0, lax.axis_index("xb"), 128, 0), (HEADS, 1, 4, 128)
    )
    q_all = exchange(jnp.broadcast_to(own.reshape(1, 64, 128), (STEPS, 64, 128)), DEPTH)
    parts = attend(q_all, (held, held_core))
    parts = exchange(parts.reshape(STEPS * HEADS, 8, 128), DEPTH + PLACE)
    attended = finish(parts.reshape(STEPS * HEADS * 8, 128))
    return jnp.dot(attended, w_out, preferred_element_type=F32).astype(BF16)


def solution(mesh):
    split = Mesh(mesh.devices.reshape(4, 2, 2, 2, 2, 4, 2), ALL)
    return jax.shard_map(
        local,
        mesh=split,
        in_specs=(P(ALL, None), P(ALL, None), P(ALL, None), P()),
        out_specs=P(ALL, None),
        check_vma=False,
    )
```

```python
import functools

import jax
import jax.numpy as jnp
from jax import lax
from jax.experimental import pallas as pl
from jax.experimental.pallas import tpu as pltpu
from jax.sharding import Mesh, PartitionSpec as P

HD = 64
HEADS = 16
STEPS = 8
ALL = ("y", "zh", "core", "xa", "xb", "zq", "zo")
PLACE = ("y", "xa", "zo")
DEPTH = ("zh", "zq")
F32 = jnp.float32
BF16 = jnp.bfloat16
VMEM = pl.BlockSpec(memory_space=pltpu.VMEM)


def iota(shape, dim):
    return lax.broadcasted_iota(jnp.int32, shape, dim)


def pack_kernel(q_ref, k_ref, v_ref, out_ref):
    low = iota((128, 128), 1) < HD
    low4 = iota((4, 128), 1) < HD
    rest = jnp.zeros((12, 128), F32)
    for pair in range(HEADS // 2):
        span = slice(pair * 128, (pair + 1) * 128)
        k = k_ref[:, span]
        v = v_ref[:, span]
        k_turned = pltpu.roll(k.astype(F32), HD, 1).astype(BF16)
        v_turned = pltpu.roll(v.astype(F32), HD, 1).astype(BF16)
        out_ref[2 * pair, 0:128, :] = jnp.where(low, k, v_turned)
        out_ref[2 * pair + 1, 0:128, :] = jnp.where(low, k_turned, v)
        q = q_ref[:, span].astype(F32)
        q_turned = pltpu.roll(q, HD, 1)
        even = jnp.where(low4, q[0:4], q_turned[4:8])
        odd = jnp.where(low4, q_turned[0:4], q[4:8])
        out_ref[2 * pair, 128:144, :] = jnp.concatenate([even, rest], 0).astype(BF16)
        out_ref[2 * pair + 1, 128:144, :] = jnp.concatenate([odd, rest], 0).astype(BF16)


def pack(q, k, v):
    return pl.pallas_call(
        pack_kernel,
        out_shape=jax.ShapeDtypeStruct((HEADS, 144, 128), BF16),
        in_specs=[VMEM, VMEM, VMEM],
        out_specs=VMEM,
        name="pack",
    )(q, k, v)


def packed_stats(level):
    level = level.T[0:8]
    first = level.astype(BF16).astype(F32)
    second = (level - first).astype(BF16).astype(F32)
    third = level - first - second
    row = iota((8, 128), 0)
    terms = jnp.where(row == 0, first, jnp.where(row == 1, second, third))
    return jnp.concatenate([terms, terms], 0).astype(BF16)


def take_queries(q_ref):
    low64 = iota((64, 128), 1) < HD
    parts = []
    for step in range(STEPS):
        pair = q_ref[step].astype(F32) * HD**-0.5
        parts.append(jnp.where(low64, pair, 0.0))
        parts.append(jnp.where(low64, pltpu.roll(pair, HD, 1), 0.0))
    return jnp.concatenate(parts, 0).astype(BF16)


def absorb(group, q, kv_refs, top, total):
    rows = group * 128
    low = iota((rows, 128), 1) < HD
    for kv_ref in kv_refs:
        for c in range(HEADS // group):
            kv = kv_ref[c * group : (c + 1) * group, 0:128, :].reshape(rows, 128)
            score = lax.dot_general(q, kv, (((1,), (1,)), ((), ())), preferred_element_type=F32)
            here = jnp.max(score, 1, keepdims=True)
            new = here if top is None else jnp.maximum(top, here)
            weights = jnp.exp(score - new).astype(BF16)
            marked = jnp.where(low, jnp.ones((), BF16), kv)
            part = jnp.dot(weights, marked, preferred_element_type=F32)
            total = part if top is None else total * jnp.exp(top - new) + part
            top = new
    return top, total


def attend_first_kernel(group, q_ref, kva_ref, kvb_ref, top_ref, total_ref):
    top, total = absorb(group, take_queries(q_ref), (kva_ref, kvb_ref), None, None)
    top_ref[...] = jnp.broadcast_to(top, top_ref.shape)
    total_ref[...] = total


def attend_second_kernel(group, q_ref, kva_ref, kvb_ref, top_ref, total_ref, out_ref):
    top, total = top_ref[:, 0:1], total_ref[...]
    top, total = absorb(group, take_queries(q_ref), (kva_ref, kvb_ref), top, total)
    low64 = iota((64, 128), 1) < HD
    for step in range(STEPS):
        span = slice(step * 128, (step + 1) * 128)
        whole = total[span]
        mixed = whole / jnp.where(iota((128, 128), 1) < HD, 1.0, pltpu.roll(whole, HD, 1))
        packed = jnp.where(low64, pltpu.roll(mixed[:64], HD, 1), mixed[64:])
        out_ref[step, 0:64, :] = packed.astype(BF16)
        out_ref[step, 64:80, :] = packed_stats(jnp.log(whole) + top[span])


def attend(kernel, shapes, q, *rest, group=2):
    queries, rows = STEPS * 128, 2 * HEADS * 128
    return pl.pallas_call(
        functools.partial(kernel, group),
        out_shape=shapes,
        in_specs=[VMEM] * (1 + len(rest)),
        out_specs=jax.tree.map(lambda shape: VMEM, shapes),
        compiler_params=pltpu.CompilerParams(vmem_limit_bytes=32 * 2**20),
        cost_estimate=pl.CostEstimate(
            flops=4 * queries * rows * 128, bytes_accessed=2**21, transcendentals=queries * rows
        ),
        name=kernel.__name__,
    )(q, *rest)


def combine_kernel(part_ref, out_ref):
    n = part_ref.shape[0]
    levels = []
    for z in range(n):
        terms = part_ref[z, 64:80, :].astype(F32)
        levels.append(terms[0:1] + terms[1:2] + terms[2:3])
    level = jnp.concatenate(levels, 0)
    weight = jnp.exp(level - jnp.max(level, 0, keepdims=True))
    weight = weight / jnp.sum(weight, 0, keepdims=True)
    weight = jnp.concatenate([weight, jnp.zeros((128 - n, 128), F32)], 0).T
    low64 = iota((64, 128), 1) < HD
    total = jnp.zeros((64, 128), F32)
    for z in range(n):
        column = weight[:, z : z + 1]
        total += jnp.where(low64, column[:64], column[64:]) * part_ref[z, 0:64, :].astype(F32)
    out_ref[...] = total.astype(BF16)


def combine(parts):
    return pl.pallas_call(
        combine_kernel,
        out_shape=jax.ShapeDtypeStruct((64, 128), BF16),
        in_specs=[VMEM],
        out_specs=VMEM,
        name="combine",
    )(parts)


def exchange(blocks, axes):
    return lax.all_to_all(blocks, axes, split_axis=0, concat_axis=0, tiled=True)


def swap(block, axis):
    return lax.ppermute(block, axis, [(0, 1), (1, 0)])


def local(queries, keys, values, w_out):
    held = exchange(pack(queries, keys, values), PLACE)
    held_x = swap(held, "xb")
    held_core = swap(held, "core")
    q_place = held[:, 128:132, :].reshape(1, 64, 128)
    q_all = exchange(jnp.broadcast_to(q_place, (STEPS, 64, 128)), DEPTH)
    held_x, q_all = lax.optimization_barrier((held_x, q_all))
    held_both = swap(held_x, "core")
    state = jax.ShapeDtypeStruct((STEPS * 128, 128), F32)
    top, total = attend(attend_first_kernel, (state, state), q_all, held, held_core)
    result = jax.ShapeDtypeStruct((STEPS, 80, 128), BF16)
    parts = attend(attend_second_kernel, result, q_all, held_x, held_both, top, total)
    attended = combine(exchange(parts, DEPTH)).reshape(HEADS, 4, 128)
    rows = exchange(attended, PLACE).reshape(HEADS, 4, 2, HD)
    rows = rows.transpose(2, 1, 0, 3).reshape(8, HEADS * HD)
    return jnp.dot(rows, w_out, preferred_element_type=F32).astype(BF16)


def solution(mesh):
    split = Mesh(mesh.devices.reshape(4, 2, 2, 2, 2, 4, 2), ALL)
    return jax.shard_map(
        local,
        mesh=split,
        in_specs=(P(ALL, None), P(ALL, None), P(ALL, None), P()),
        out_specs=P(ALL, None),
        check_vma=False,
    )
```

```python
import functools

import jax
import jax.numpy as jnp
from jax import lax
from jax.experimental import pallas as pl
from jax.experimental.pallas import tpu as pltpu
from jax.sharding import Mesh, PartitionSpec as P

HD = 64
HEADS = 16
STEPS = 8
ALL = ("y", "zh", "core", "xa", "xb", "zq", "zo")
PLACE = ("y", "xa", "zo")
DEPTH = ("zh", "zq")
F32 = jnp.float32
BF16 = jnp.bfloat16
VMEM = pl.BlockSpec(memory_space=pltpu.VMEM)


def iota(shape, dim):
    return lax.broadcasted_iota(jnp.int32, shape, dim)


def pack_kernel(q_ref, k_ref, v_ref, out_ref):
    low = iota((128, 128), 1) < HD
    low4 = iota((4, 128), 1) < HD
    rest = jnp.zeros((12, 128), F32)
    for pair in range(HEADS // 2):
        span = slice(pair * 128, (pair + 1) * 128)
        k = k_ref[:, span]
        v = v_ref[:, span]
        k_turned = pltpu.roll(k.astype(F32), HD, 1).astype(BF16)
        v_turned = pltpu.roll(v.astype(F32), HD, 1).astype(BF16)
        out_ref[2 * pair, 0:128, :] = jnp.where(low, k, v_turned)
        out_ref[2 * pair + 1, 0:128, :] = jnp.where(low, k_turned, v)
        q = q_ref[:, span].astype(F32)
        q_turned = pltpu.roll(q, HD, 1)
        even = jnp.where(low4, q[0:4], q_turned[4:8])
        odd = jnp.where(low4, q_turned[0:4], q[4:8])
        out_ref[2 * pair, 128:144, :] = jnp.concatenate([even, rest], 0).astype(BF16)
        out_ref[2 * pair + 1, 128:144, :] = jnp.concatenate([odd, rest], 0).astype(BF16)


def pack(q, k, v):
    return pl.pallas_call(
        pack_kernel,
        out_shape=jax.ShapeDtypeStruct((HEADS, 144, 128), BF16),
        in_specs=[VMEM, VMEM, VMEM],
        out_specs=VMEM,
        name="pack",
    )(q, k, v)


def take_queries(q_ref):
    low64 = iota((64, 128), 1) < HD
    parts = []
    for step in range(STEPS):
        pair = q_ref[step].astype(F32) * HD**-0.5
        parts.append(jnp.where(low64, pair, 0.0))
        parts.append(jnp.where(low64, pltpu.roll(pair, HD, 1), 0.0))
    return jnp.concatenate(parts, 0).astype(BF16)


def absorb(group, q, kv_refs, top, total):
    rows = group * 128
    low = iota((rows, 128), 1) < HD
    for kv_ref in kv_refs:
        for c in range(HEADS // group):
            kv = kv_ref[c * group : (c + 1) * group, 0:128, :].reshape(rows, 128)
            score = lax.dot_general(q, kv, (((1,), (1,)), ((), ())), preferred_element_type=F32)
            here = jnp.max(score, 1, keepdims=True)
            new = here if top is None else jnp.maximum(top, here)
            weights = jnp.exp(score - new).astype(BF16)
            marked = jnp.where(low, jnp.ones((), BF16), kv)
            part = jnp.dot(weights, marked, preferred_element_type=F32)
            total = part if top is None else total * jnp.exp(top - new) + part
            top = new
    return top, total


def attend_first_kernel(group, q_ref, kva_ref, kvb_ref, top_ref, total_ref):
    top, total = absorb(group, take_queries(q_ref), (kva_ref, kvb_ref), None, None)
    top_ref[...] = jnp.broadcast_to(top, top_ref.shape)
    total_ref[...] = total


def attend_second_kernel(group, q_ref, kva_ref, kvb_ref, top_ref, total_ref, out_ref):
    top, total = jnp.max(top_ref[...], 1, keepdims=True), total_ref[...]
    top, total = absorb(group, take_queries(q_ref), (kva_ref, kvb_ref), top, total)
    low64 = iota((64, 128), 1) < HD
    sub = iota((64, 128), 0) % 8 < 4
    first_half = iota((64, 128), 1) % HD < HD // 2
    for step in range(STEPS):
        a = total[step * 128 : step * 128 + 64]
        b = total[step * 128 + 64 : step * 128 + 128]
        weight = jnp.where(low64, a, pltpu.roll(b, HD, 1))
        mixed = jnp.where(low64, pltpu.roll(a, HD, 1), b) / weight
        highest = jnp.where(
            low64, top[step * 128 : step * 128 + 64], top[step * 128 + 64 : step * 128 + 128]
        )
        level = jnp.log(weight) + highest
        first = level.astype(BF16).astype(F32)
        level = jnp.where(first_half, first, level - first)
        mixed_turned = pltpu.roll(mixed.reshape(8, 8, 128), 4, 1).reshape(64, 128)
        level_turned = pltpu.roll(level.reshape(8, 8, 128), 4, 1).reshape(64, 128)
        even = jnp.where(sub, mixed, level_turned).reshape(8, 8, 128)
        odd = jnp.where(sub, mixed_turned, level).reshape(8, 8, 128)
        both = jnp.stack([even, odd], 1).reshape(128, 128)
        out_ref[step * 128 : (step + 1) * 128, :] = both.astype(BF16)


def attend(kernel, shapes, q, *rest, group=2):
    queries, rows = STEPS * 128, 2 * HEADS * 128
    return pl.pallas_call(
        functools.partial(kernel, group),
        out_shape=shapes,
        in_specs=[VMEM] * (1 + len(rest)),
        out_specs=jax.tree.map(lambda shape: VMEM, shapes),
        compiler_params=pltpu.CompilerParams(vmem_limit_bytes=32 * 2**20),
        cost_estimate=pl.CostEstimate(
            flops=4 * queries * rows * 128, bytes_accessed=2**21, transcendentals=queries * rows
        ),
        name=kernel.__name__,
    )(q, *rest)


def finish_kernel(part_ref, w_ref, out_ref):
    near = iota((HEADS * 8, 128), 1) % HD < HD // 2
    blocks, levels = [], []
    for step in range(STEPS):
        block = part_ref[step * HEADS * 8 : (step + 1) * HEADS * 8, :].astype(F32)
        other = jnp.where(near, pltpu.roll(block, 96, 1), pltpu.roll(block, 32, 1))
        level = (block + other).reshape(HEADS, 8, 128)
        blocks.append(block.reshape(HEADS, 8, 128))
        levels.append(pltpu.roll(level, 4, 1))
    top = functools.reduce(jnp.maximum, levels)
    weights = [jnp.exp(level - top) for level in levels]
    mixed = sum(w * b for w, b in zip(weights, blocks)) / sum(weights)
    turned = pltpu.roll(mixed, HD, 2)
    low = iota((8, 128), 1) < HD
    upper = iota((8, 128), 0) < 4
    tiles = []
    for pair in range(HEADS // 2):
        head = jnp.where(low, mixed[2 * pair], turned[2 * pair + 1])
        tail = jnp.where(low, turned[2 * pair], mixed[2 * pair + 1])
        tiles.append(jnp.where(upper, head, pltpu.roll(tail, 4, 0)))
    rows = jnp.concatenate(tiles, 1).astype(BF16)
    out_ref[...] = jnp.dot(rows, w_ref[...], preferred_element_type=F32).astype(BF16)


def finish(parts, w_out):
    return pl.pallas_call(
        finish_kernel,
        out_shape=jax.ShapeDtypeStruct((8, HEADS * HD), BF16),
        in_specs=[VMEM, VMEM],
        out_specs=VMEM,
        name="finish",
    )(parts, w_out)


def exchange(blocks, axes):
    return lax.all_to_all(blocks, axes, split_axis=0, concat_axis=0, tiled=True)


def swap(block, axis):
    return lax.ppermute(block, axis, [(0, 1), (1, 0)])


def local(queries, keys, values, w_out):
    held = exchange(pack(queries, keys, values), PLACE)
    held_x = swap(held, "xb")
    held_core = swap(held, "core")
    q_place = held[:, 128:132, :].reshape(1, 64, 128)
    q_all = exchange(jnp.broadcast_to(q_place, (STEPS, 64, 128)), DEPTH)
    held_x, q_all = lax.optimization_barrier((held_x, q_all))
    held_both = swap(held_x, "core")
    state = jax.ShapeDtypeStruct((STEPS * 128, 128), F32)
    top, total = attend(attend_first_kernel, (state, state), q_all, held, held_core)
    result = jax.ShapeDtypeStruct((STEPS * 128, 128), BF16)
    parts = attend(attend_second_kernel, result, q_all, held_x, held_both, top, total)
    parts = exchange(parts.reshape(STEPS * HEADS, 8, 128), DEPTH + PLACE)
    return finish(parts.reshape(STEPS * HEADS * 8, 128), w_out)


def solution(mesh):
    split = Mesh(mesh.devices.reshape(4, 2, 2, 2, 2, 4, 2), ALL)
    return jax.shard_map(
        local,
        mesh=split,
        in_specs=(P(ALL, None), P(ALL, None), P(ALL, None), P()),
        out_specs=P(ALL, None),
        check_vma=False,
    )
```

```python
import functools

import jax
import jax.numpy as jnp
from jax import lax
from jax.experimental import pallas as pl
from jax.experimental.pallas import tpu as pltpu
from jax.sharding import Mesh, PartitionSpec as P

HD = 64
HEADS = 16
STEPS = 8
ALL = ("y", "zh", "core", "xa", "xb", "zq", "zo")
PLACE = ("y", "xa", "zo")
DEPTH = ("zh", "zq")
F32 = jnp.float32
BF16 = jnp.bfloat16
VMEM = pl.BlockSpec(memory_space=pltpu.VMEM)


def iota(shape, dim):
    return lax.broadcasted_iota(jnp.int32, shape, dim)


def pack_kernel(q_ref, k_ref, v_ref, out_ref):
    low = iota((128, 128), 1) < HD
    low4 = iota((4, 128), 1) < HD
    rest = jnp.zeros((12, 128), F32)
    for pair in range(HEADS // 2):
        span = slice(pair * 128, (pair + 1) * 128)
        k = k_ref[:, span]
        v = v_ref[:, span]
        k_turned = pltpu.roll(k.astype(F32), HD, 1).astype(BF16)
        v_turned = pltpu.roll(v.astype(F32), HD, 1).astype(BF16)
        out_ref[2 * pair, 0:128, :] = jnp.where(low, k, v_turned)
        out_ref[2 * pair + 1, 0:128, :] = jnp.where(low, k_turned, v)
        q = q_ref[:, span].astype(F32)
        q_turned = pltpu.roll(q, HD, 1)
        even = jnp.where(low4, q[0:4], q_turned[4:8])
        odd = jnp.where(low4, q_turned[0:4], q[4:8])
        out_ref[2 * pair, 128:144, :] = jnp.concatenate([even, rest], 0).astype(BF16)
        out_ref[2 * pair + 1, 128:144, :] = jnp.concatenate([odd, rest], 0).astype(BF16)


def pack(q, k, v):
    return pl.pallas_call(
        pack_kernel,
        out_shape=jax.ShapeDtypeStruct((HEADS, 144, 128), BF16),
        in_specs=[VMEM, VMEM, VMEM],
        out_specs=VMEM,
        name="pack",
    )(q, k, v)


def take_queries(q_ref):
    low64 = iota((64, 128), 1) < HD
    parts = []
    for step in range(STEPS):
        pair = q_ref[step].astype(F32) * HD**-0.5
        parts.append(jnp.where(low64, pair, 0.0))
        parts.append(jnp.where(low64, pltpu.roll(pair, HD, 1), 0.0))
    return jnp.concatenate(parts, 0).astype(BF16)


def absorb(group, q, kv_refs, top, total):
    rows = group * 128
    low = iota((rows, 128), 1) < HD
    for kv_ref in kv_refs:
        for c in range(HEADS // group):
            kv = kv_ref[c * group : (c + 1) * group, 0:128, :].reshape(rows, 128)
            score = lax.dot_general(q, kv, (((1,), (1,)), ((), ())), preferred_element_type=F32)
            here = jnp.max(score, 1, keepdims=True)
            new = here if top is None else jnp.maximum(top, here)
            weights = jnp.exp(score - new).astype(BF16)
            marked = jnp.where(low, jnp.ones((), BF16), kv)
            part = jnp.dot(weights, marked, preferred_element_type=F32)
            total = part if top is None else total * jnp.exp(top - new) + part
            top = new
    return top, total


def attend_first_kernel(group, q_ref, kva_ref, kvb_ref, top_ref, total_ref):
    top, total = absorb(group, take_queries(q_ref), (kva_ref, kvb_ref), None, None)
    top_ref[...] = jnp.broadcast_to(top, top_ref.shape)
    total_ref[...] = total


def attend_second_kernel(group, q_ref, kva_ref, kvb_ref, top_ref, total_ref, out_ref):
    top, total = jnp.max(top_ref[...], 1, keepdims=True), total_ref[...]
    top, total = absorb(group, take_queries(q_ref), (kva_ref, kvb_ref), top, total)
    low64 = iota((64, 128), 1) < HD
    sub = iota((64, 128), 0) % 8 < 4
    first_half = iota((64, 128), 1) % HD < HD // 2
    for step in range(STEPS):
        a = total[step * 128 : step * 128 + 64]
        b = total[step * 128 + 64 : step * 128 + 128]
        weight = jnp.where(low64, a, pltpu.roll(b, HD, 1))
        mixed = jnp.where(low64, pltpu.roll(a, HD, 1), b) / weight
        highest = jnp.where(
            low64, top[step * 128 : step * 128 + 64], top[step * 128 + 64 : step * 128 + 128]
        )
        level = jnp.log(weight) + highest
        first = level.astype(BF16).astype(F32)
        level = jnp.where(first_half, first, level - first)
        mixed_turned = pltpu.roll(mixed.reshape(8, 8, 128), 4, 1).reshape(64, 128)
        level_turned = pltpu.roll(level.reshape(8, 8, 128), 4, 1).reshape(64, 128)
        even = jnp.where(sub, mixed, level_turned).reshape(8, 8, 128)
        odd = jnp.where(sub, mixed_turned, level).reshape(8, 8, 128)
        both = jnp.stack([even, odd], 1).reshape(128, 128)
        out_ref[step * 128 : (step + 1) * 128, :] = both.astype(BF16)


def attend(kernel, shapes, q, *rest, group=2):
    queries, rows = STEPS * 128, 2 * HEADS * 128
    return pl.pallas_call(
        functools.partial(kernel, group),
        out_shape=shapes,
        in_specs=[VMEM] * (1 + len(rest)),
        out_specs=jax.tree.map(lambda shape: VMEM, shapes),
        compiler_params=pltpu.CompilerParams(vmem_limit_bytes=32 * 2**20),
        cost_estimate=pl.CostEstimate(
            flops=4 * queries * rows * 128, bytes_accessed=2**21, transcendentals=queries * rows
        ),
        name=kernel.__name__,
    )(q, *rest)


def finish_kernel(part_ref, w_ref, out_ref):
    near = iota((HEADS * 8, 128), 1) % HD < HD // 2
    blocks, levels = [], []
    for step in range(STEPS):
        block = part_ref[step * HEADS * 8 : (step + 1) * HEADS * 8, :].astype(F32)
        other = jnp.where(near, pltpu.roll(block, 96, 1), pltpu.roll(block, 32, 1))
        level = (block + other).reshape(HEADS, 8, 128)
        blocks.append(block.reshape(HEADS, 8, 128))
        levels.append(pltpu.roll(level, 4, 1))
    top = functools.reduce(jnp.maximum, levels)
    weights = [jnp.exp(level - top) for level in levels]
    mixed = sum(w * b for w, b in zip(weights, blocks)) / sum(weights)
    turned = pltpu.roll(mixed, HD, 2)
    low = iota((8, 128), 1) < HD
    upper = iota((8, 128), 0) < 4
    tiles = []
    for pair in range(HEADS // 2):
        head = jnp.where(low, mixed[2 * pair], turned[2 * pair + 1])
        tail = jnp.where(low, turned[2 * pair], mixed[2 * pair + 1])
        tiles.append(jnp.where(upper, head, pltpu.roll(tail, 4, 0)))
    rows = jnp.concatenate(tiles, 1).astype(BF16)
    out_ref[...] = jnp.dot(rows, w_ref[...], preferred_element_type=F32).astype(BF16)


def finish(parts, w_out):
    return pl.pallas_call(
        finish_kernel,
        out_shape=jax.ShapeDtypeStruct((8, HEADS * HD), BF16),
        in_specs=[VMEM, VMEM],
        out_specs=VMEM,
        name="finish",
    )(parts, w_out)


def exchange(blocks, axes):
    return lax.all_to_all(blocks, axes, split_axis=0, concat_axis=0, tiled=True)


def swap(block, axis):
    return lax.ppermute(block, axis, [(0, 1), (1, 0)])


def local(queries, keys, values, w_out):
    held = exchange(pack(queries, keys, values), PLACE)
    held_x = swap(held, "xb")
    held_core = swap(held, "core")
    q_place = held[:, 128:132, :].reshape(1, 64, 128)
    q_all = exchange(jnp.broadcast_to(q_place, (STEPS, 64, 128)), DEPTH)
    held_both = lax.ppermute(held, ("core", "xb"), [(0, 3), (1, 2), (2, 1), (3, 0)])
    state = jax.ShapeDtypeStruct((STEPS * 128, 128), F32)
    top, total = attend(attend_first_kernel, (state, state), q_all, held, held_x)
    result = jax.ShapeDtypeStruct((STEPS * 128, 128), BF16)
    parts = attend(attend_second_kernel, result, q_all, held_core, held_both, top, total)
    parts = exchange(parts.reshape(STEPS * HEADS, 8, 128), DEPTH + PLACE)
    return finish(parts.reshape(STEPS * HEADS * 8, 128), w_out)


def solution(mesh):
    split = Mesh(mesh.devices.reshape(4, 2, 2, 2, 2, 4, 2), ALL)
    return jax.shard_map(
        local,
        mesh=split,
        in_specs=(P(ALL, None), P(ALL, None), P(ALL, None), P()),
        out_specs=P(ALL, None),
        check_vma=False,
    )
```

```python
import functools

import jax
import jax.numpy as jnp
from jax import lax
from jax.experimental import pallas as pl
from jax.experimental.pallas import tpu as pltpu
from jax.sharding import Mesh, PartitionSpec as P

HD = 64
HEADS = 16
STEPS = 8
ALL = ("y", "zh", "core", "xa", "xb", "zq", "zo")
PLACE = ("zo", "xa", "y")
DEPTH = ("zh", "zq")
F32 = jnp.float32
BF16 = jnp.bfloat16
VMEM = pl.BlockSpec(memory_space=pltpu.VMEM)


def iota(shape, dim):
    return lax.broadcasted_iota(jnp.int32, shape, dim)


def pack_kernel(q_ref, k_ref, v_ref, out_ref):
    low = iota((128, 128), 1) < HD
    low4 = iota((4, 128), 1) < HD
    rest = jnp.zeros((12, 128), F32)
    for pair in range(HEADS // 2):
        span = slice(pair * 128, (pair + 1) * 128)
        k = k_ref[:, span]
        v = v_ref[:, span]
        k_turned = pltpu.roll(k.astype(F32), HD, 1).astype(BF16)
        v_turned = pltpu.roll(v.astype(F32), HD, 1).astype(BF16)
        out_ref[2 * pair, 0:128, :] = jnp.where(low, k, v_turned)
        out_ref[2 * pair + 1, 0:128, :] = jnp.where(low, k_turned, v)
        q = q_ref[:, span].astype(F32)
        q_turned = pltpu.roll(q, HD, 1)
        even = jnp.where(low4, q[0:4], q_turned[4:8])
        odd = jnp.where(low4, q_turned[0:4], q[4:8])
        out_ref[2 * pair, 128:144, :] = jnp.concatenate([even, rest], 0).astype(BF16)
        out_ref[2 * pair + 1, 128:144, :] = jnp.concatenate([odd, rest], 0).astype(BF16)


def pack(q, k, v):
    return pl.pallas_call(
        pack_kernel,
        out_shape=jax.ShapeDtypeStruct((HEADS, 144, 128), BF16),
        in_specs=[VMEM, VMEM, VMEM],
        out_specs=VMEM,
        name="pack",
    )(q, k, v)


def take_queries(q_ref):
    low64 = iota((64, 128), 1) < HD
    parts = []
    for step in range(STEPS):
        pair = q_ref[step].astype(F32) * HD**-0.5
        parts.append(jnp.where(low64, pair, 0.0))
        parts.append(jnp.where(low64, pltpu.roll(pair, HD, 1), 0.0))
    return jnp.concatenate(parts, 0).astype(BF16)


def absorb(group, q, kv_refs, top, total):
    rows = group * 128
    low = iota((rows, 128), 1) < HD
    for kv_ref in kv_refs:
        for c in range(HEADS // group):
            kv = kv_ref[c * group : (c + 1) * group, 0:128, :].reshape(rows, 128)
            score = lax.dot_general(q, kv, (((1,), (1,)), ((), ())), preferred_element_type=F32)
            here = jnp.max(score, 1, keepdims=True)
            new = here if top is None else jnp.maximum(top, here)
            weights = jnp.exp(score - new).astype(BF16)
            marked = jnp.where(low, jnp.ones((), BF16), kv)
            part = jnp.dot(weights, marked, preferred_element_type=F32)
            total = part if top is None else total * jnp.exp(top - new) + part
            top = new
    return top, total


def attend_first_kernel(group, q_ref, kva_ref, kvb_ref, top_ref, total_ref):
    top, total = absorb(group, take_queries(q_ref), (kva_ref, kvb_ref), None, None)
    top_ref[...] = jnp.broadcast_to(top, top_ref.shape)
    total_ref[...] = total


def attend_second_kernel(group, q_ref, kva_ref, kvb_ref, top_ref, total_ref, out_ref):
    top, total = jnp.max(top_ref[...], 1, keepdims=True), total_ref[...]
    top, total = absorb(group, take_queries(q_ref), (kva_ref, kvb_ref), top, total)
    low64 = iota((64, 128), 1) < HD
    sub = iota((64, 128), 0) % 8 < 4
    first_half = iota((64, 128), 1) % HD < HD // 2
    for step in range(STEPS):
        a = total[step * 128 : step * 128 + 64]
        b = total[step * 128 + 64 : step * 128 + 128]
        weight = jnp.where(low64, a, pltpu.roll(b, HD, 1))
        mixed = jnp.where(low64, pltpu.roll(a, HD, 1), b) / weight
        highest = jnp.where(
            low64, top[step * 128 : step * 128 + 64], top[step * 128 + 64 : step * 128 + 128]
        )
        level = jnp.log(weight) + highest
        first = level.astype(BF16).astype(F32)
        level = jnp.where(first_half, first, level - first)
        mixed_turned = pltpu.roll(mixed.reshape(8, 8, 128), 4, 1).reshape(64, 128)
        level_turned = pltpu.roll(level.reshape(8, 8, 128), 4, 1).reshape(64, 128)
        even = jnp.where(sub, mixed, level_turned).reshape(8, 8, 128)
        odd = jnp.where(sub, mixed_turned, level).reshape(8, 8, 128)
        both = jnp.stack([even, odd], 1).reshape(128, 128)
        out_ref[step * 128 : (step + 1) * 128, :] = both.astype(BF16)


def attend(kernel, shapes, q, *rest, group=2):
    queries, rows = STEPS * 128, 2 * HEADS * 128
    return pl.pallas_call(
        functools.partial(kernel, group),
        out_shape=shapes,
        in_specs=[VMEM] * (1 + len(rest)),
        out_specs=jax.tree.map(lambda shape: VMEM, shapes),
        compiler_params=pltpu.CompilerParams(vmem_limit_bytes=32 * 2**20),
        cost_estimate=pl.CostEstimate(
            flops=4 * queries * rows * 128, bytes_accessed=2**21, transcendentals=queries * rows
        ),
        name=kernel.__name__,
    )(q, *rest)


def finish_kernel(part_ref, w_ref, out_ref):
    near = iota((HEADS * 8, 128), 1) % HD < HD // 2
    blocks, levels = [], []
    for step in range(STEPS):
        block = part_ref[step * HEADS * 8 : (step + 1) * HEADS * 8, :].astype(F32)
        other = jnp.where(near, pltpu.roll(block, 96, 1), pltpu.roll(block, 32, 1))
        level = (block + other).reshape(HEADS, 8, 128)
        blocks.append(block.reshape(HEADS, 8, 128))
        levels.append(pltpu.roll(level, 4, 1))
    top = functools.reduce(jnp.maximum, levels)
    weights = [jnp.exp(level - top) for level in levels]
    mixed = sum(w * b for w, b in zip(weights, blocks)) / sum(weights)
    turned = pltpu.roll(mixed, HD, 2)
    low = iota((8, 128), 1) < HD
    upper = iota((8, 128), 0) < 4
    tiles = []
    for pair in range(HEADS // 2):
        head = jnp.where(low, mixed[2 * pair], turned[2 * pair + 1])
        tail = jnp.where(low, turned[2 * pair], mixed[2 * pair + 1])
        tiles.append(jnp.where(upper, head, pltpu.roll(tail, 4, 0)))
    rows = jnp.concatenate(tiles, 1).astype(BF16)
    out_ref[...] = jnp.dot(rows, w_ref[...], preferred_element_type=F32).astype(BF16)


def finish(parts, w_out):
    return pl.pallas_call(
        finish_kernel,
        out_shape=jax.ShapeDtypeStruct((8, HEADS * HD), BF16),
        in_specs=[VMEM, VMEM],
        out_specs=VMEM,
        name="finish",
    )(parts, w_out)


def exchange(blocks, axes):
    return lax.all_to_all(blocks, axes, split_axis=0, concat_axis=0, tiled=True)


def swap(block, axis):
    return lax.ppermute(block, axis, [(0, 1), (1, 0)])


def local(queries, keys, values, w_out):
    held = exchange(pack(queries, keys, values), PLACE)
    held_x = swap(held, "xb")
    held_core = swap(held, "core")
    q_place = held[:, 128:132, :].reshape(1, 64, 128)
    q_all = exchange(jnp.broadcast_to(q_place, (STEPS, 64, 128)), DEPTH)
    held_x, q_all = lax.optimization_barrier((held_x, q_all))
    held_both = swap(held_x, "core")
    state = jax.ShapeDtypeStruct((STEPS * 128, 128), F32)
    top, total = attend(attend_first_kernel, (state, state), q_all, held, held_core)
    result = jax.ShapeDtypeStruct((STEPS * 128, 128), BF16)
    parts = attend(attend_second_kernel, result, q_all, held_x, held_both, top, total)
    parts = exchange(parts.reshape(STEPS * HEADS, 8, 128), DEPTH + PLACE)
    return finish(parts.reshape(STEPS * HEADS * 8, 128), w_out)


def solution(mesh):
    split = Mesh(mesh.devices.reshape(4, 2, 2, 2, 2, 4, 2), ALL)
    return jax.shard_map(
        local,
        mesh=split,
        in_specs=(P(ALL, None), P(ALL, None), P(ALL, None), P()),
        out_specs=P(ALL, None),
        check_vma=False,
    )
```

```python
import functools

import jax
import jax.numpy as jnp
from jax import lax
from jax.experimental import pallas as pl
from jax.experimental.pallas import tpu as pltpu
from jax.sharding import Mesh, PartitionSpec as P

HD = 64
HEADS = 16
STEPS = 8
ALL = ("y", "zh", "core", "xa", "xb", "zq", "zo")
PLACE = ("zo", "xa", "y")
DEPTH = ("zh", "zq")
F32 = jnp.float32
BF16 = jnp.bfloat16
VMEM = pl.BlockSpec(memory_space=pltpu.VMEM)


def iota(shape, dim):
    return lax.broadcasted_iota(jnp.int32, shape, dim)


def pack_kernel(q_ref, k_ref, v_ref, out_ref):
    low = iota((128, 128), 1) < HD
    low4 = iota((4, 128), 1) < HD
    rest = jnp.zeros((12, 128), F32)
    for pair in range(HEADS // 2):
        span = slice(pair * 128, (pair + 1) * 128)
        k = k_ref[:, span]
        v = v_ref[:, span]
        k_turned = pltpu.roll(k.astype(F32), HD, 1).astype(BF16)
        v_turned = pltpu.roll(v.astype(F32), HD, 1).astype(BF16)
        out_ref[2 * pair, 0:128, :] = jnp.where(low, k, v_turned)
        out_ref[2 * pair + 1, 0:128, :] = jnp.where(low, k_turned, v)
        q = q_ref[:, span].astype(F32)
        q_turned = pltpu.roll(q, HD, 1)
        even = jnp.where(low4, q[0:4], q_turned[4:8])
        odd = jnp.where(low4, q_turned[0:4], q[4:8])
        out_ref[2 * pair, 128:144, :] = jnp.concatenate([even, rest], 0).astype(BF16)
        out_ref[2 * pair + 1, 128:144, :] = jnp.concatenate([odd, rest], 0).astype(BF16)


def pack(q, k, v):
    return pl.pallas_call(
        pack_kernel,
        out_shape=jax.ShapeDtypeStruct((HEADS, 144, 128), BF16),
        in_specs=[VMEM, VMEM, VMEM],
        out_specs=VMEM,
        name="pack",
    )(q, k, v)


def take_queries(q_ref):
    low64 = iota((64, 128), 1) < HD
    parts = []
    for step in range(STEPS):
        pair = q_ref[step].astype(F32) * HD**-0.5
        parts.append(jnp.where(low64, pair, 0.0))
        parts.append(jnp.where(low64, pltpu.roll(pair, HD, 1), 0.0))
    return jnp.concatenate(parts, 0).astype(BF16)


def absorb(group, q, kv_refs, top, total):
    rows = group * 128
    low = iota((rows, 128), 1) < HD
    for kv_ref in kv_refs:
        for c in range(HEADS // group):
            kv = kv_ref[c * group : (c + 1) * group, 0:128, :].reshape(rows, 128)
            score = lax.dot_general(q, kv, (((1,), (1,)), ((), ())), preferred_element_type=F32)
            here = jnp.max(score, 1, keepdims=True)
            new = here if top is None else jnp.maximum(top, here)
            weights = jnp.exp(score - new).astype(BF16)
            marked = jnp.where(low, jnp.ones((), BF16), kv)
            part = jnp.dot(weights, marked, preferred_element_type=F32)
            total = part if top is None else total * jnp.exp(top - new) + part
            top = new
    return top, total


def attend_first_kernel(group, q_ref, kva_ref, kvb_ref, top_ref, total_ref):
    top, total = absorb(group, take_queries(q_ref), (kva_ref, kvb_ref), None, None)
    top_ref[...] = jnp.broadcast_to(top, top_ref.shape)
    total_ref[...] = total


def attend_second_kernel(group, q_ref, kva_ref, kvb_ref, top_ref, total_ref, out_ref):
    top, total = jnp.max(top_ref[...], 1, keepdims=True), total_ref[...]
    top, total = absorb(group, take_queries(q_ref), (kva_ref, kvb_ref), top, total)
    low64 = iota((64, 128), 1) < HD
    sub = iota((64, 128), 0) % 8 < 4
    first_half = iota((64, 128), 1) % HD < HD // 2
    for step in range(STEPS):
        a = total[step * 128 : step * 128 + 64]
        b = total[step * 128 + 64 : step * 128 + 128]
        weight = jnp.where(low64, a, pltpu.roll(b, HD, 1))
        mixed = jnp.where(low64, pltpu.roll(a, HD, 1), b) / weight
        highest = jnp.where(
            low64, top[step * 128 : step * 128 + 64], top[step * 128 + 64 : step * 128 + 128]
        )
        level = jnp.log(weight) + highest
        first = level.astype(BF16).astype(F32)
        level = jnp.where(first_half, first, level - first)
        mixed_turned = pltpu.roll(mixed.reshape(8, 8, 128), 4, 1).reshape(64, 128)
        level_turned = pltpu.roll(level.reshape(8, 8, 128), 4, 1).reshape(64, 128)
        even = jnp.where(sub, mixed, level_turned).reshape(8, 8, 128)
        odd = jnp.where(sub, mixed_turned, level).reshape(8, 8, 128)
        both = jnp.stack([even, odd], 1).reshape(128, 128)
        out_ref[step * 128 : (step + 1) * 128, :] = both.astype(BF16)


def attend(kernel, shapes, q, *rest, group=2):
    queries, rows = STEPS * 128, 2 * HEADS * 128
    return pl.pallas_call(
        functools.partial(kernel, group),
        out_shape=shapes,
        in_specs=[VMEM] * (1 + len(rest)),
        out_specs=jax.tree.map(lambda shape: VMEM, shapes),
        compiler_params=pltpu.CompilerParams(vmem_limit_bytes=20 * 2**20),
        cost_estimate=pl.CostEstimate(
            flops=4 * queries * rows * 128, bytes_accessed=2**21, transcendentals=queries * rows
        ),
        name=kernel.__name__,
    )(q, *rest)


def finish_kernel(part_ref, w_ref, out_ref):
    near = iota((HEADS * 8, 128), 1) % HD < HD // 2
    blocks, levels = [], []
    for step in range(STEPS):
        block = part_ref[step * HEADS * 8 : (step + 1) * HEADS * 8, :].astype(F32)
        other = jnp.where(near, pltpu.roll(block, 96, 1), pltpu.roll(block, 32, 1))
        level = (block + other).reshape(HEADS, 8, 128)
        blocks.append(block.reshape(HEADS, 8, 128))
        levels.append(pltpu.roll(level, 4, 1))
    top = functools.reduce(jnp.maximum, levels)
    weights = [jnp.exp(level - top) for level in levels]
    mixed = sum(w * b for w, b in zip(weights, blocks)) / sum(weights)
    turned = pltpu.roll(mixed, HD, 2)
    low = iota((8, 128), 1) < HD
    upper = iota((8, 128), 0) < 4
    tiles = []
    for pair in range(HEADS // 2):
        head = jnp.where(low, mixed[2 * pair], turned[2 * pair + 1])
        tail = jnp.where(low, turned[2 * pair], mixed[2 * pair + 1])
        tiles.append(jnp.where(upper, head, pltpu.roll(tail, 4, 0)))
    rows = jnp.concatenate(tiles, 1).astype(BF16)
    out_ref[...] = jnp.dot(rows, w_ref[...], preferred_element_type=F32).astype(BF16)


def finish(parts, w_out):
    return pl.pallas_call(
        finish_kernel,
        out_shape=jax.ShapeDtypeStruct((8, HEADS * HD), BF16),
        in_specs=[VMEM, VMEM],
        out_specs=VMEM,
        compiler_params=pltpu.CompilerParams(vmem_limit_bytes=8 * 2**20),
        name="finish",
    )(parts, w_out)


def exchange(blocks, axes):
    return lax.all_to_all(blocks, axes, split_axis=0, concat_axis=0, tiled=True)


def swap(block, axis):
    return lax.ppermute(block, axis, [(0, 1), (1, 0)])


def local(queries, keys, values, w_out):
    held = exchange(pack(queries, keys, values), PLACE)
    held_x = swap(held, "xb")
    held_core = swap(held, "core")
    q_place = held[:, 128:132, :].reshape(1, 64, 128)
    q_all = exchange(jnp.broadcast_to(q_place, (STEPS, 64, 128)), DEPTH)
    held_x, q_all = lax.optimization_barrier((held_x, q_all))
    held_both = swap(held_x, "core")
    state = jax.ShapeDtypeStruct((STEPS * 128, 128), F32)
    top, total = attend(attend_first_kernel, (state, state), q_all, held, held_core)
    result = jax.ShapeDtypeStruct((STEPS * 128, 128), BF16)
    parts = attend(attend_second_kernel, result, q_all, held_x, held_both, top, total)
    parts = exchange(parts.reshape(STEPS * HEADS, 8, 128), DEPTH + PLACE)
    return finish(parts.reshape(STEPS * HEADS * 8, 128), w_out)


def solution(mesh):
    split = Mesh(mesh.devices.reshape(4, 2, 2, 2, 2, 4, 2), ALL)
    return jax.shard_map(
        local,
        mesh=split,
        in_specs=(P(ALL, None), P(ALL, None), P(ALL, None), P()),
        out_specs=P(ALL, None),
        check_vma=False,
    )
```

```python
import functools

import jax
import jax.numpy as jnp
from jax import lax
from jax.experimental import pallas as pl
from jax.experimental.pallas import tpu as pltpu
from jax.sharding import Mesh, PartitionSpec as P

HD = 64
HEADS = 16
STEPS = 8
ALL = ("y", "zh", "core", "xa", "xb", "zq", "zo")
PLACE = ("zo", "xa", "y")
DEPTH = ("zh", "zq")
F32 = jnp.float32
BF16 = jnp.bfloat16
VMEM = pl.BlockSpec(memory_space=pltpu.VMEM)


def iota(shape, dim):
    return lax.broadcasted_iota(jnp.int32, shape, dim)


def pack_kernel(q_ref, k_ref, v_ref, out_ref):
    low = iota((128, 128), 1) < HD
    low4 = iota((4, 128), 1) < HD
    rest = jnp.zeros((12, 128), F32)
    for pair in range(HEADS // 2):
        span = slice(pair * 128, (pair + 1) * 128)
        k = k_ref[:, span]
        v = v_ref[:, span]
        k_turned = pltpu.roll(k.astype(F32), HD, 1).astype(BF16)
        v_turned = pltpu.roll(v.astype(F32), HD, 1).astype(BF16)
        out_ref[2 * pair, 0:128, :] = jnp.where(low, k, v_turned)
        out_ref[2 * pair + 1, 0:128, :] = jnp.where(low, k_turned, v)
        q = q_ref[:, span].astype(F32)
        q_turned = pltpu.roll(q, HD, 1)
        even = jnp.where(low4, q[0:4], q_turned[4:8])
        odd = jnp.where(low4, q_turned[0:4], q[4:8])
        out_ref[2 * pair, 128:144, :] = jnp.concatenate([even, rest], 0).astype(BF16)
        out_ref[2 * pair + 1, 128:144, :] = jnp.concatenate([odd, rest], 0).astype(BF16)


def pack(q, k, v):
    return pl.pallas_call(
        pack_kernel,
        out_shape=jax.ShapeDtypeStruct((HEADS, 144, 128), BF16),
        in_specs=[VMEM, VMEM, VMEM],
        out_specs=VMEM,
        name="pack",
    )(q, k, v)


def take_queries(q_ref):
    low64 = iota((64, 128), 1) < HD
    parts = []
    for step in range(STEPS):
        pair = q_ref[step].astype(F32) * HD**-0.5
        parts.append(jnp.where(low64, pair, 0.0))
        parts.append(jnp.where(low64, pltpu.roll(pair, HD, 1), 0.0))
    return jnp.concatenate(parts, 0).astype(BF16)


def mark(kv):
    return jnp.where(iota(kv.shape, 1) < HD, jnp.ones((), BF16), kv)


def mark_kernel(kv_ref, out_ref):
    for source in range(HEADS):
        out_ref[source] = mark(kv_ref[source, 0:128, :])


def mark_all(kv):
    return pl.pallas_call(
        mark_kernel,
        out_shape=jax.ShapeDtypeStruct((HEADS, 128, 128), BF16),
        in_specs=[VMEM],
        out_specs=VMEM,
        compiler_params=pltpu.CompilerParams(vmem_limit_bytes=8 * 2**20),
        cost_estimate=pl.CostEstimate(flops=2**33, bytes_accessed=2**20, transcendentals=0),
        name="mark",
    )(kv)


def absorb(group, q, pairs, top, total):
    rows = group * 128
    for kv_ref, marked_ref in pairs:
        for c in range(HEADS // group):
            kv = kv_ref[c * group : (c + 1) * group, 0:128, :].reshape(rows, 128)
            score = lax.dot_general(q, kv, (((1,), (1,)), ((), ())), preferred_element_type=F32)
            here = jnp.max(score, 1, keepdims=True)
            new = here if top is None else jnp.maximum(top, here)
            weights = jnp.exp(score - new).astype(BF16)
            if marked_ref is None:
                marked = mark(kv)
            else:
                marked = marked_ref[c * group : (c + 1) * group].reshape(rows, 128)
            part = jnp.dot(weights, marked, preferred_element_type=F32)
            total = part if top is None else total * jnp.exp(top - new) + part
            top = new
    return top, total


def attend_first_kernel(group, q_ref, kva_ref, kvb_ref, top_ref, total_ref):
    top, total = absorb(group, take_queries(q_ref), ((kva_ref, None), (kvb_ref, None)), None, None)
    top_ref[...] = jnp.broadcast_to(top, top_ref.shape)
    total_ref[...] = total


def attend_second_kernel(group, q_ref, kva_ref, marked_ref, kvb_ref, top_ref, total_ref, out_ref):
    top, total = jnp.max(top_ref[...], 1, keepdims=True), total_ref[...]
    top, total = absorb(group, take_queries(q_ref), ((kva_ref, marked_ref), (kvb_ref, None)), top, total)
    low64 = iota((64, 128), 1) < HD
    sub = iota((64, 128), 0) % 8 < 4
    first_half = iota((64, 128), 1) % HD < HD // 2
    for step in range(STEPS):
        a = total[step * 128 : step * 128 + 64]
        b = total[step * 128 + 64 : step * 128 + 128]
        weight = jnp.where(low64, a, pltpu.roll(b, HD, 1))
        mixed = jnp.where(low64, pltpu.roll(a, HD, 1), b) / weight
        highest = jnp.where(
            low64, top[step * 128 : step * 128 + 64], top[step * 128 + 64 : step * 128 + 128]
        )
        level = jnp.log(weight) + highest
        first = level.astype(BF16).astype(F32)
        level = jnp.where(first_half, first, level - first)
        mixed_turned = pltpu.roll(mixed.reshape(8, 8, 128), 4, 1).reshape(64, 128)
        level_turned = pltpu.roll(level.reshape(8, 8, 128), 4, 1).reshape(64, 128)
        even = jnp.where(sub, mixed, level_turned).reshape(8, 8, 128)
        odd = jnp.where(sub, mixed_turned, level).reshape(8, 8, 128)
        both = jnp.stack([even, odd], 1).reshape(128, 128)
        out_ref[step * 128 : (step + 1) * 128, :] = both.astype(BF16)


def attend(kernel, shapes, q, *rest, group=2):
    queries, rows = STEPS * 128, 2 * HEADS * 128
    return pl.pallas_call(
        functools.partial(kernel, group),
        out_shape=shapes,
        in_specs=[VMEM] * (1 + len(rest)),
        out_specs=jax.tree.map(lambda shape: VMEM, shapes),
        compiler_params=pltpu.CompilerParams(vmem_limit_bytes=20 * 2**20),
        cost_estimate=pl.CostEstimate(
            flops=4 * queries * rows * 128, bytes_accessed=2**21, transcendentals=queries * rows
        ),
        name=kernel.__name__,
    )(q, *rest)


def finish_kernel(part_ref, w_ref, out_ref):
    near = iota((HEADS * 8, 128), 1) % HD < HD // 2
    blocks, levels = [], []
    for step in range(STEPS):
        block = part_ref[step * HEADS * 8 : (step + 1) * HEADS * 8, :].astype(F32)
        other = jnp.where(near, pltpu.roll(block, 96, 1), pltpu.roll(block, 32, 1))
        level = (block + other).reshape(HEADS, 8, 128)
        blocks.append(block.reshape(HEADS, 8, 128))
        levels.append(pltpu.roll(level, 4, 1))
    top = functools.reduce(jnp.maximum, levels)
    weights = [jnp.exp(level - top) for level in levels]
    mixed = sum(w * b for w, b in zip(weights, blocks)) / sum(weights)
    turned = pltpu.roll(mixed, HD, 2)
    low = iota((8, 128), 1) < HD
    upper = iota((8, 128), 0) < 4
    tiles = []
    for pair in range(HEADS // 2):
        head = jnp.where(low, mixed[2 * pair], turned[2 * pair + 1])
        tail = jnp.where(low, turned[2 * pair], mixed[2 * pair + 1])
        tiles.append(jnp.where(upper, head, pltpu.roll(tail, 4, 0)))
    rows = jnp.concatenate(tiles, 1).astype(BF16)
    out_ref[...] = jnp.dot(rows, w_ref[...], preferred_element_type=F32).astype(BF16)


def finish(parts, w_out):
    return pl.pallas_call(
        finish_kernel,
        out_shape=jax.ShapeDtypeStruct((8, HEADS * HD), BF16),
        in_specs=[VMEM, VMEM],
        out_specs=VMEM,
        compiler_params=pltpu.CompilerParams(vmem_limit_bytes=8 * 2**20),
        name="finish",
    )(parts, w_out)


def exchange(blocks, axes):
    return lax.all_to_all(blocks, axes, split_axis=0, concat_axis=0, tiled=True)


def swap(block, axis):
    return lax.ppermute(block, axis, [(0, 1), (1, 0)])


def local(queries, keys, values, w_out):
    held = exchange(pack(queries, keys, values), PLACE)
    held_x = swap(held, "xb")
    held_core = swap(held, "core")
    q_place = held[:, 128:132, :].reshape(1, 64, 128)
    q_all = exchange(jnp.broadcast_to(q_place, (STEPS, 64, 128)), DEPTH)
    marked_x = mark_all(held_x)
    held_x, marked_x = lax.optimization_barrier((held_x, marked_x))
    held_both = swap(held_x, "core")
    state = jax.ShapeDtypeStruct((STEPS * 128, 128), F32)
    top, total = attend(attend_first_kernel, (state, state), q_all, held, held_core)
    result = jax.ShapeDtypeStruct((STEPS * 128, 128), BF16)
    parts = attend(attend_second_kernel, result, q_all, held_x, marked_x, held_both, top, total)
    parts = exchange(parts.reshape(STEPS * HEADS, 8, 128), DEPTH + PLACE)
    return finish(parts.reshape(STEPS * HEADS * 8, 128), w_out)


def solution(mesh):
    split = Mesh(mesh.devices.reshape(4, 2, 2, 2, 2, 4, 2), ALL)
    return jax.shard_map(
        local,
        mesh=split,
        in_specs=(P(ALL, None), P(ALL, None), P(ALL, None), P()),
        out_specs=P(ALL, None),
        check_vma=False,
    )
```
